512 devices in a mesh: row: 16 (over y_hi, x), col: 32 (over z, y_lo, core).
Axes of the slice: x: 4, y: 8 (y_hi: 4, y_lo: 2; y = y_hi * 2 + y_lo), z: 8, core: 2. Of those that a mesh axis runs over, the one named last changes fastest.
Arguments:
- hidden_act: bfloat16 [2048, 28672], P('row', 'col'), may hold values from -0.14941406 to 0.14941406
- out_grad: bfloat16 [2048, 8192], P('col', 'row'), may hold values from -6 to 6
- weight: bfloat16 [28672, 8192], P('col', 'row'), may hold values from -0.03125 to 0.03125
- loss_mask: int32 [2048], replicated, may hold values from 0 to 1
- positions: int32 [2048], replicated, may hold values from 0 to 255, as said below
Outputs:
- input_grad: bfloat16 [2048, 28672], P('row', 'col')
- weight_grad: bfloat16 [28672, 8192], P('col', 'row')
The draws below stay inside these ranges and needn't reach their ends.
Inputs may be any that keep to these rules, and one draw needn't show every extreme that they name: positions is 0 at the first token and otherwise either 0 or one more than the previous token's; no document is longer than min(512, 256) tokens.
All inputs are finite; a program needn't handle non-finite values.
Results may differ from the reference program's by a relative error of at most 0.019.
Values may be sent and summed in bfloat16 or wider, within the bound.
A program may use at most 64 MiB of HBM per device.

```python
import jax
import jax.numpy as jnp
from jax import lax

D = 8192
FF = 28672
TOKENS = 2048
N_ROW = 16


def document_layout(key):
    layout_key = jax.random.fold_in(key, 5)
    extra_key, place_key = jax.random.split(layout_key)
    indices = jnp.arange(TOKENS, dtype=jnp.int32)
    span = min(TOKENS // 4, 256)
    short_len = max(2, span // 32)
    extra = (jax.random.randint(extra_key, (TOKENS,), 0, max(2, span // 4)) == 0) & (indices >= span)
    short_start = jax.random.randint(place_key, (), span, TOKENS - short_len + 1).astype(jnp.int32)
    starting = extra | (indices % span == 0) | (indices == short_start) | (indices == short_start + short_len)
    return (starting, short_start, short_len)


def draw_positions(key, part):
    starting, short_start, short_len = document_layout(key)
    indices = jnp.arange(TOKENS, dtype=jnp.int32)
    latest = lax.cummax(jnp.where(starting, indices, 0).astype(jnp.int32), axis=0)
    return (indices - latest).astype(jnp.int32)


def draw_loss_mask(key, part):
    starting, short_start, short_len = document_layout(key)
    key = jax.random.fold_in(key, 11)
    start_key, length_key = jax.random.split(key)
    indices = jnp.arange(TOKENS, dtype=jnp.int32)
    span = min(TOKENS // 4, 256)
    span_count = max(1, TOKENS // 512)
    longest = max(3, span // 16)
    span_starts = jax.random.randint(start_key, (span_count,), 0, TOKENS).astype(jnp.int32)
    span_lengths = jax.random.randint(length_key, (span_count,), 2, longest + 1).astype(jnp.int32)
    inside = (indices[None, :] >= span_starts[:, None]) & (indices[None, :] < span_starts[:, None] + span_lengths[:, None])
    in_spans = jnp.any(inside, axis=0)
    in_short = (indices >= short_start) & (indices < short_start + short_len)
    return jnp.where(in_spans | in_short, 0, 1).astype(jnp.int32)


def levels(rng, dims, shards, smallest, largest):
    loudness = 1.0
    for position, parts in shards:
        steps = jax.random.uniform(jax.random.fold_in(jax.random.fold_in(rng, 6), position), (parts,), jnp.float32, smallest / len(shards), largest / len(shards))
        loudness = loudness * jnp.repeat(jnp.exp(steps), dims[position] // parts).reshape((-1,) + (1,) * (len(dims) - 1 - position))
    return loudness


def normal_values(stream_key, shape, deviation, bound, cuts=(), held_as=jnp.bfloat16):
    drawn = deviation * jax.random.normal(stream_key, shape, jnp.float32)
    if cuts:
        drawn = drawn * levels(stream_key, shape, cuts, -0.22, 0.18)
    return jnp.clip(drawn, -bound, bound).astype(held_as)


def setup_inputs(seed: int = 0) -> dict:
    arg_keys = jax.random.split(jax.random.key(seed), 6)
    hidden_act = normal_values(arg_keys[0], (TOKENS, FF), 0.025, 0.14941406, ((0, 16), (1, 32)))
    out_grad = normal_values(arg_keys[1], (TOKENS, D), 1.0, 6.0, ((0, 32), (1, 16)))
    weight = normal_values(arg_keys[2], (FF, D), FF ** -0.5, 0.03125, ((0, 32), (1, 16)))
    loss_mask = draw_loss_mask(jax.random.fold_in(arg_keys[5], 71), 0)
    positions = draw_positions(jax.random.fold_in(arg_keys[5], 71), 0)
    return {"hidden_act": hidden_act, "out_grad": out_grad, "weight": weight, "loss_mask": loss_mask, "positions": positions}


def token_weights(loss_mask, positions):
    count_all = positions.shape[0]
    indices = jnp.arange(count_all, dtype=jnp.int32)
    doc_first = (indices - positions).astype(jnp.int32)
    boundary = jnp.where(positions == 0, indices, count_all).astype(jnp.int32)
    following = jnp.concatenate([boundary[1:], jnp.full((1,), count_all, jnp.int32)])
    doc_end = lax.cummin(following, axis=0, reverse=True).astype(jnp.int32)
    kept_prefix = jnp.concatenate([jnp.zeros((1,), jnp.int32), jnp.cumsum(loss_mask).astype(jnp.int32)])
    kept_counts = jnp.maximum(kept_prefix[doc_end] - kept_prefix[doc_first], 1)
    doc_lengths = doc_end - doc_first
    return loss_mask.astype(jnp.float32) * doc_lengths.astype(jnp.float32) / kept_counts.astype(jnp.float32)


def reference(hidden_act, out_grad, weight, loss_mask, positions):
    token_scale = token_weights(loss_mask, positions)
    scaled_grad = (out_grad.astype(jnp.float32) * token_scale[:, None]).astype(jnp.bfloat16)
    width_block = D // N_ROW

    def add_block(running, block_index):
        grad_cols = lax.dynamic_slice_in_dim(scaled_grad, block_index * width_block, width_block, 1)
        weight_cols = lax.dynamic_slice_in_dim(weight, block_index * width_block, width_block, 1)
        partial_block = lax.dot_general(grad_cols, weight_cols, (((1,), (1,)), ((), ())), preferred_element_type=jnp.float32)
        rounded = lax.optimization_barrier(partial_block.astype(jnp.bfloat16))
        return running + rounded.astype(jnp.float32), None

    initial = jnp.zeros((TOKENS, FF), jnp.float32)
    summed, unused = lax.scan(add_block, initial, jnp.arange(N_ROW, dtype=jnp.int32))
    input_grad = summed.astype(jnp.bfloat16)
    weight_grad = lax.dot_general(hidden_act, scaled_grad, (((0,), (0,)), ((), ())), preferred_element_type=jnp.float32)
    return input_grad, weight_grad.astype(jnp.bfloat16)
```

```python
import jax
import jax.numpy as jnp
from jax import lax
from jax.experimental import pallas as pl
from jax.experimental.pallas import tpu as pltpu
from jax.sharding import PartitionSpec as P

MESH = pl.DeviceIdType.MESH
BF16 = jnp.bfloat16
F32 = jnp.float32
NY, NX, NZ = 4, 4, 8
CH = 4


def local_token_scale(mask_ref, pos_ref, col, n_local):
    rows = pos_ref.shape[0]
    lane = lax.broadcasted_iota(jnp.int32, (n_local, 128), 1)
    sub = lax.broadcasted_iota(jnp.int32, (n_local, 128), 0)
    per = 128 // n_local
    mine_row = col // per
    offset = (col % per) * n_local
    pick = lane == sub + offset
    mine_pos = pos_ref[pl.ds(mine_row, 1), :]
    mine_mask = mask_ref[pl.ds(mine_row, 1), :]
    first = jnp.sum(jnp.where(pick, (mine_row * 128 + lane - mine_pos).astype(F32), 0.0), axis=1, keepdims=True)
    own_mask = jnp.sum(jnp.where(pick, mine_mask.astype(F32), 0.0), axis=1, keepdims=True)
    length = jnp.zeros((n_local, 128), F32)
    kept = jnp.zeros((n_local, 128), F32)
    for q in range(rows):
        begins = (q * 128 + lane - pos_ref[q : q + 1, :]).astype(F32)
        same = begins == first
        length = length + jnp.where(same, 1.0, 0.0)
        kept = kept + jnp.where(same, mask_ref[q : q + 1, :].astype(F32), 0.0)
    length = jnp.sum(length, axis=1, keepdims=True)
    kept = jnp.maximum(jnp.sum(kept, axis=1, keepdims=True), 1.0)
    return own_mask * length / kept


def dot_nn(a, b):
    return lax.dot_general(a, b, (((1,), (0,)), ((), ())), preferred_element_type=F32)


def dot_nt(a, b):
    return lax.dot_general(a, b, (((1,), (1,)), ((), ())), preferred_element_type=F32)


def kernel(
    hid_ref, og_ref, w_ref, mask_ref, pos_ref, ig_ref, wg_ref,
    sc, hidt, S, wrecv, wg_send, wg_recv, wg_own, ig_send, ig_recv, ig_own, igy_send, igy_recv,
    sc_s, sc_r, hy_s, hy_r, hx_s, hx_r, w_s, w_r, z_s, z_r, k_s, k_r, wg_s, wg_r, ig_s, ig_r, iy_s, iy_r,
):
    row = lax.axis_index("row")
    col = lax.axis_index("col")
    Y, x = row // NX, row % NX
    z, l, k = col // 4, (col // 2) % 2, col % 2
    dpx = x + 1 - 2 * (x % 2)
    tpx = 3 - x
    par, tpar = x // 2, 1 - x // 2
    g = ((x + 1) // 2) % 2
    lt = (z % 2 + g) % 2

    def dev(Y=Y, x=x, z=z, l=l, k=k):
        return (Y * NX + x, z * 4 + l * 2 + k)

    dp, tp, other = dev(x=dpx), dev(x=tpx), dev(k=1 - k)
    zdev = (dev(z=(z + 1) % NZ), dev(z=(z + NZ - 1) % NZ))
    ydev = [dev(Y=(Y + d) % NY) for d in range(NY)]
    ldev, dpl = dev(l=1 - l), dev(x=dpx, l=1 - l)

    bar = pltpu.get_barrier_semaphore()
    peers = [dp, tp, other, *zdev, *ydev[1:], ldev, dpl]
    for p in peers:
        pl.semaphore_signal(bar, inc=1, device_id=p, device_id_type=MESH)

    def rc(src, dst, ss, rs, to):
        return pltpu.make_async_remote_copy(src, dst, ss, rs, device_id=to, device_id_type=MESH)

    scale = local_token_scale(mask_ref, pos_ref, col, og_ref.shape[0])
    sc[...] = (og_ref[...].astype(F32) * scale).astype(BF16)
    myj = 2 * Y + par
    hidt[myj] = hid_ref[...].T

    pl.semaphore_wait(bar, len(peers))

    member = l == lt
    a_far = rc(sc, S.at[z, k, 1], sc_s.at[0], sc_r.at[1], dp)
    b_far = rc(sc, S.at[z, k, 1], sc_s.at[1], sc_r.at[1], dpl)
    b_near = rc(sc, S.at[z, k, 0], sc_s.at[1], sc_r.at[0], ldev)

    @pl.when(member)
    def _():
        b_near.start()
        S[z, k, 0] = sc[...]

    @pl.when(jnp.logical_not(member))
    def _():
        a_far.start()
        b_far.start()

    hy = [rc(hidt.at[myj], hidt.at[myj], hy_s.at[d], hy_r.at[d], ydev[d]) for d in range(1, NY)]
    hx = [None] * NY

    def send_hx(d):
        j = 2 * ((Y + NY - d) % NY) + par
        hx[d] = rc(hidt.at[j], hidt.at[j], hx_s.at[d], hx_r.at[d], tp)
        hx[d].start()

    wc = rc(w_ref, wrecv, w_s.at[0], w_r.at[0], dp)
    hy[0].start()
    hy[2].start()
    send_hx(0)
    hy[1].start()
    wc.start()

    @pl.when(jnp.logical_not(member))
    def _():
        b_near.wait_recv()

    a_far.wait_recv()

    kc = []

    def to_core(zz, slot, idx):
        c = rc(S.at[zz, k, slot], S.at[zz, k, slot], k_s.at[idx], k_r.at[idx], other)
        c.start()
        kc.append(c)

    zc = {}

    def z_send(direction, step, slot):
        origin = (z + NZ - step) % NZ if direction == 0 else (z + step) % NZ
        i = (direction * 4 + step) * 2 + slot
        c = rc(S.at[origin, k, slot], S.at[origin, k, slot], z_s.at[i], z_r.at[i], zdev[direction])
        c.start()
        zc[direction, step, slot] = c

    for slot in range(2):
        for direction in range(2):
            z_send(direction, 0, slot)
    for slot in range(2):
        to_core(z, slot, slot)
    n = 2
    for step in range(1, 5):
        for slot in range(2):
            for direction in range(2):
                if step == 4 and slot != direction:
                    continue
                zc[direction, step - 1, slot].wait_recv()
                if step < 3 or (step == 3 and slot == direction):
                    z_send(direction, step, slot)
                origin = (z + NZ - step) % NZ if direction == 0 else (z + step) % NZ
                to_core(origin, slot, n)
                n += 1
        if step == 2:
            hy[0].wait_recv()
            send_hx(1)
            hy[2].wait_recv()
            send_hx(3)
    hy[1].wait_recv()
    send_hx(2)
    for c in kc:
        c.wait_recv()
    wc.wait_recv()

    def ig_block(d, parity):
        zz = 2 * ((Y + d) % NY) + parity
        s0 = S[zz, :, 0].reshape(128, -1)
        s1 = S[zz, :, 1].reshape(128, -1)
        return dot_nt(s0, w_ref[...]) + dot_nt(s1, wrecv[...])

    order = (2, 1, 3, 0)
    igc = {}
    for d in order:
        ig_send[d] = ig_block(d, tpar).astype(BF16)
        igc[d] = rc(ig_send.at[d], ig_recv.at[d], ig_s.at[d], ig_r.at[d], tp)
        igc[d].start()

    for d in range(NY):
        hx[d].wait_recv()
    rows = hid_ref.shape[1] // CH
    wgc = []

    def lhs(c):
        return jnp.concatenate([hidt[j, c * rows : (c + 1) * rows] for j in range(2 * NY)], axis=1)

    def rhs(slot):
        return S[:, :, slot].reshape(1024, -1)

    for c in range(CH):
        sl = pl.ds(c * rows, rows)
        wg_send[sl] = dot_nn(lhs(c), rhs(1)).astype(BF16)
        cp = rc(wg_send.at[sl], wg_recv.at[sl], wg_s.at[c], wg_r.at[c], dp)
        cp.start()
        wgc.append(cp)
    for d in order:
        ig_own[d] = ig_block(d, par)
    for c in range(CH):
        wg_own[c * rows : (c + 1) * rows] = dot_nn(lhs(c), rhs(0))

    iyc = {}
    for d in order:
        igc[d].wait_recv()
        total = ig_own[d] + ig_recv[d].astype(F32)
        if d:
            igy_send[d] = total.astype(BF16)
            iyc[d] = rc(igy_send.at[d], igy_recv.at[d], iy_s.at[d], iy_r.at[d], ydev[d])
            iyc[d].start()
        else:
            ig_own[0] = total
    for c in range(CH):
        wgc[c].wait_recv()
        sl = pl.ds(c * rows, rows)
        wg_ref[sl] = (wg_own[sl] + wg_recv[sl].astype(F32)).astype(BF16)
    for d in (1, 3, 2):
        iyc[d].wait_recv()
    ig_ref[...] = (
        ig_own[0] + igy_recv[1].astype(F32) + igy_recv[2].astype(F32) + igy_recv[3].astype(F32)
    ).astype(BF16)

    b_near.wait_send()

    @pl.when(jnp.logical_not(member))
    def _():
        a_far.wait_send()

    for c in [*hy, *hx, wc, *zc.values(), *kc, *igc.values(), *wgc, *iyc.values()]:
        c.wait_send()


def on_device(hidden_act, out_grad, weight, loss_mask, positions):
    t, f = hidden_act.shape
    n, b = out_grad.shape
    dma = pltpu.SemaphoreType.DMA
    vm = pltpu.VMEM
    return pl.pallas_call(
        kernel,
        out_shape=(jax.ShapeDtypeStruct((t, f), BF16), jax.ShapeDtypeStruct((f, b), BF16)),
        in_specs=[pl.BlockSpec(memory_space=vm)] * 5,
        out_specs=[pl.BlockSpec(memory_space=vm)] * 2,
        scratch_shapes=[
            vm((n, b), BF16),
            vm((8, f, t), BF16),
            vm((NZ, 2, 2, n, b), BF16),
            vm((f, b), BF16),
            vm((f, b), BF16),
            vm((f, b), BF16),
            vm((f, b), F32),
            vm((NY, t, f), BF16),
            vm((NY, t, f), BF16),
            vm((NY, t, f), F32),
            vm((NY, t, f), BF16),
            vm((NY, t, f), BF16),
            dma((2,)), dma((2,)),
            dma((4,)), dma((4,)),
            dma((4,)), dma((4,)),
            dma((1,)), dma((1,)),
            dma((16,)), dma((16,)),
            dma((16,)), dma((16,)),
            dma((CH,)), dma((CH,)),
            dma((4,)), dma((4,)),
            dma((4,)), dma((4,)),
        ],
        compiler_params=pltpu.CompilerParams(
            collective_id=0, has_side_effects=True, vmem_limit_bytes=48 * 2**20
        ),
    )(hidden_act, out_grad, weight, loss_mask.reshape(-1, 128), positions.reshape(-1, 128))


def solution(mesh):
    return jax.shard_map(
        on_device,
        mesh=mesh,
        in_specs=(P("row", "col"), P("col", "row"), P("col", "row"), P(), P()),
        out_specs=(P("row", "col"), P("col", "row")),
        check_vma=False,
    )
```

```python
import contextlib

import jax
import jax.numpy as jnp
from jax import lax
from jax.experimental import pallas as pl
from jax.experimental.pallas import tpu as pltpu
from jax.sharding import PartitionSpec as P

MESH = pl.DeviceIdType.MESH
BF16 = jnp.bfloat16
F32 = jnp.float32
NY, NX, NZ = 4, 4, 8
scope = contextlib.nullcontext
VMEM_LIMIT = 62 * 2**20
SUB = 2
LAST_HF = 4
CH = 4


def local_token_scale(mask_ref, pos_ref, col, n_local):
    rows = pos_ref.shape[0]
    lane = lax.broadcasted_iota(jnp.int32, (n_local, 128), 1)
    sub = lax.broadcasted_iota(jnp.int32, (n_local, 128), 0)
    per = 128 // n_local
    mine_row = col // per
    offset = (col % per) * n_local
    pick = lane == sub + offset
    mine_pos = pos_ref[pl.ds(mine_row, 1), :]
    mine_mask = mask_ref[pl.ds(mine_row, 1), :]
    first = jnp.sum(jnp.where(pick, (mine_row * 128 + lane - mine_pos).astype(F32), 0.0), axis=1, keepdims=True)
    own_mask = jnp.sum(jnp.where(pick, mine_mask.astype(F32), 0.0), axis=1, keepdims=True)
    length = jnp.zeros((n_local, 128), F32)
    kept = jnp.zeros((n_local, 128), F32)
    for q in range(rows):
        begins = (q * 128 + lane - pos_ref[q : q + 1, :]).astype(F32)
        same = begins == first
        length = length + jnp.where(same, 1.0, 0.0)
        kept = kept + jnp.where(same, mask_ref[q : q + 1, :].astype(F32), 0.0)
    length = jnp.sum(length, axis=1, keepdims=True)
    kept = jnp.maximum(jnp.sum(kept, axis=1, keepdims=True), 1.0)
    return own_mask * length / kept


def dot_nn(a, b):
    return lax.dot_general(a, b, (((1,), (0,)), ((), ())), preferred_element_type=F32)


def dot_nt(a, b):
    return lax.dot_general(a, b, (((1,), (1,)), ((), ())), preferred_element_type=F32)


def kernel(
    hid_hbm, og_hbm, w_hbm, mask_hbm, pos_hbm, ig_ref, wg_ref,
    hid_ref, og_ref, w_ref, mask_ref, pos_ref,
    sc, hidt, S, wrecv, wg_send, wg_recv, wg_own, ig_send, ig_recv, ig_own, a_send, a_recv, b_send, b_recv,
    in_s, sc_s, sc_r, hy_s, hy_r, hx_s, hx_r, w_s, w_r, z_s, z_r, k_s, k_r, wg_s, wg_r, ig_s, ig_r, a_s, a_r, b_s, b_r,
):
    row = lax.axis_index("row")
    col = lax.axis_index("col")
    Y, x = row // NX, row % NX
    z, l, k = col // 4, (col // 2) % 2, col % 2
    dpx = x + 1 - 2 * (x % 2)
    tpx = 3 - x
    par, tpar = x // 2, 1 - x // 2
    g = ((x + 1) // 2) % 2
    lt = (z % 2 + g) % 2

    def dev(Y=Y, x=x, z=z, l=l, k=k):
        return (Y * NX + x, z * 4 + l * 2 + k)

    dp, tp, other = dev(x=dpx), dev(x=tpx), dev(k=1 - k)
    zdev = (dev(z=(z + 1) % NZ), dev(z=(z + NZ - 1) % NZ))
    ydev = (dev(Y=(Y + 1) % NY), dev(Y=(Y + NY - 1) % NY))
    ldev, dpl = dev(l=1 - l), dev(x=dpx, l=1 - l)

    bar = pltpu.get_barrier_semaphore()
    peers = [dp, tp, other, *zdev, *ydev, ldev, dpl]
    for p in peers:
        pl.semaphore_signal(bar, inc=1, device_id=p, device_id_type=MESH)
    load = [
        pltpu.make_async_copy(a, b, in_s.at[i])
        for i, (a, b) in enumerate(
            [(mask_hbm, mask_ref), (pos_hbm, pos_ref), (og_hbm, og_ref), (hid_hbm, hid_ref), (w_hbm, w_ref)]
        )
    ]
    for c in load:
        c.start()

    sends = []

    def rc(src, dst, ss, rs, to):
        return pltpu.make_async_remote_copy(src, dst, ss, rs, device_id=to, device_id_type=MESH)

    def go(src, dst, ss, rs, to):
        c = rc(src, dst, ss, rs, to)
        c.start()
        sends.append(c)
        return c

    for c in load[:3]:
        c.wait()
    scale = local_token_scale(mask_ref, pos_ref, col, og_ref.shape[0])
    sc[...] = (og_ref[...].astype(F32) * scale).astype(BF16)
    pl.semaphore_wait(bar, len(peers))

    member = l == lt
    a_far = rc(sc, S.at[z, k, 1], sc_s.at[0], sc_r.at[1], dp)
    b_far = rc(sc, S.at[z, k, 1], sc_s.at[1], sc_r.at[1], dpl)
    b_near = rc(sc, S.at[z, k, 0], sc_s.at[1], sc_r.at[0], ldev)

    @pl.when(member)
    def _():
        b_near.start()
        S[z, k, 0] = sc[...]

    @pl.when(jnp.logical_not(member))
    def _():
        a_far.start()
        b_far.start()

    wc = go(w_hbm, wrecv, w_s.at[0], w_r.at[0], dp)
    myj = 2 * Y + par
    half = hid_ref.shape[1] // 2
    load[3].wait()
    hidt[myj] = hid_ref[...].T

    def hrows(j, h):
        return hidt.at[j, pl.ds(h * half, half)]

    def block_of(d, parity):
        return 2 * ((Y + d) % NY) + parity

    hy, hx, hf = {}, {}, {}

    def send_hx(d, h):
        r = hrows(block_of(d, par), h)
        hx[d, h] = go(r, r, hx_s.at[d * 2 + h], hx_r.at[d * 2 + h], tp)

    for h in range(2):
        for e in range(2):
            hy[e, h] = go(hrows(myj, h), hrows(myj, h), hy_s.at[e * 2 + h], hy_r.at[e * 2 + h], ydev[e])
    send_hx(0, 0)
    send_hx(0, 1)

    def y_arrived(e, h):
        hy[e, h].wait_recv()
        if h == e:
            r = hrows(block_of((NY - 1, 1)[e], par), h)
            hf[e] = go(r, r, hy_s.at[4 + e], hy_r.at[4 + e], ydev[e])
        send_hx((NY - 1, 1)[e], h)

    a_far.wait_recv()

    kc, zc = {}, {}

    def to_core(zz, slot, idx):
        kc[idx, slot] = go(S.at[zz, k, slot], S.at[zz, k, slot], k_s.at[idx * 2 + slot], k_r.at[idx * 2 + slot], other)

    def origin_of(e, step):
        return (z + NZ - step) % NZ if e == 0 else (z + step) % NZ

    part = S.shape[3] // SUB

    def z_send(e, step, slot, u):
        i = ((e * 4 + step) * 2 + slot) * SUB + u
        r = S.at[origin_of(e, step), k, slot, pl.ds(u * part, part)]
        zc[e, step, slot, u] = go(r, r, z_s.at[i], z_r.at[i], zdev[e])

    for slot in (1, 0):
        if slot == 0:

            @pl.when(jnp.logical_not(member))
            def _():
                b_near.wait_recv()

        for u in range(SUB):
            for e in range(2):
                z_send(e, 0, slot, u)
    for slot in (1, 0):
        to_core(z, slot, 0)
    for step in range(1, 5):
        for slot in (1, 0):
            for u in range(SUB):
                for e in range(2):
                    if step == 4 and slot == e:
                        continue
                    zc[e, step - 1, slot, u].wait_recv()
                    if step < 3 or (step == 3 and slot != e):
                        z_send(e, step, slot, u)
                    if u == SUB - 1:
                        to_core(origin_of(e, step), slot, step if e == 0 or step == 4 else 4 + step)
        if step == 1:
            y_arrived(0, 0)
            y_arrived(1, 0)
        if step == 2:
            y_arrived(0, 1)
            y_arrived(1, 1)
        if step == LAST_HF:
            for e in range(2):
                hf[e].wait_recv()
                send_hx(2, e)
    for slot in (1, 0):
        for i in range(8):
            kc[i, slot].wait_recv()

    load[4].wait()
    wc.wait_recv()

    def ig_block(d, parity):
        zz = block_of(d, parity)
        s0 = S[zz, :, 0].reshape(128, -1)
        s1 = S[zz, :, 1].reshape(128, -1)
        return dot_nt(s0, w_ref[...]) + dot_nt(s1, wrecv[...])

    igc, wgc = {}, {}

    def ig_partner(d):
        with scope(f"igp{d}"):
            ig_send[d] = ig_block(d, tpar).astype(BF16)

    def send_ig(d, h):
        r = pl.ds(h * 64, 64)
        igc[d, h] = go(ig_send.at[d, r], ig_recv.at[d, r], ig_s.at[d * 2 + h], ig_r.at[d * 2 + h], tp)

    rows = hid_ref.shape[1] // CH

    def lhs(c):
        return jnp.concatenate([hidt[j, c * rows : (c + 1) * rows] for j in range(2 * NY)], axis=1)

    def rhs(slot):
        return S[:, :, slot].reshape(1024, -1)

    def wg_partner(c):
        sl = pl.ds(c * rows, rows)
        with scope(f"wgp{c}"):
            wg_send[sl] = dot_nn(lhs(c), rhs(1)).astype(BF16)
        wgc[c] = go(wg_send.at[sl], wg_recv.at[sl], wg_s.at[c], wg_r.at[c], dp)

    ig_partner(2)
    send_ig(2, 0)
    send_ig(2, 1)
    for d in range(NY):
        hx[d, 0].wait_recv()
    for c in range(CH // 2):
        wg_partner(c)
    ig_partner(1)
    send_ig(1, 1)
    ig_partner(3)
    send_ig(3, 0)
    send_ig(1, 0)
    send_ig(3, 1)
    for d in range(NY):
        hx[d, 1].wait_recv()
    for c in range(CH // 2, CH):
        wg_partner(c)
    ig_partner(0)
    send_ig(0, 0)
    send_ig(0, 1)
    for d in (2, 1, 3, 0):
        ig_own[d] = ig_block(d, par)
    for c in range(CH):
        wg_own[c * rows : (c + 1) * rows] = dot_nn(lhs(c), rhs(0))

    ac, bc = {}, {}

    def arrived(d, h):
        igc[d, h].wait_recv()
        r = pl.ds(h * 64, 64)
        return ig_own[d, r] + ig_recv[d, r].astype(F32)

    def send_b(e, h, value):
        r = pl.ds(h * 64, 64)
        b_send[e, r] = value.astype(BF16)
        bc[e, h] = go(b_send.at[e, r], b_recv.at[e, r], b_s.at[e * 2 + h], b_r.at[e * 2 + h], ydev[e])

    def wg_done(c):
        wgc[c].wait_recv()
        sl = pl.ds(c * rows, rows)
        wg_ref[sl] = (wg_own[sl] + wg_recv[sl].astype(F32)).astype(BF16)

    for e in range(2):
        a_send[e] = arrived(2, e).astype(BF16)
        ac[e] = go(a_send.at[e], a_recv.at[e], a_s.at[e], a_r.at[e], ydev[e])
    send_b(0, 1, arrived(1, 1))
    send_b(1, 0, arrived(3, 0))
    t = arrived(1, 0)
    ac[0].wait_recv()
    send_b(0, 0, t + a_recv[0].astype(F32))
    t = arrived(3, 1)
    ac[1].wait_recv()
    send_b(1, 1, t + a_recv[1].astype(F32))
    for c in range(CH - 1):
        wg_done(c)
    for h in range(2):
        ig_own[0, h * 64 : (h + 1) * 64] = arrived(0, h)
    wg_done(CH - 1)
    for h in range(2):
        for e in range(2):
            bc[e, h].wait_recv()
        r = pl.ds(h * 64, 64)
        ig_ref[r] = (ig_own[0, r] + b_recv[0, r].astype(F32) + b_recv[1, r].astype(F32)).astype(BF16)

    b_near.wait_send()

    @pl.when(jnp.logical_not(member))
    def _():
        a_far.wait_send()

    for c in sends:
        c.wait_send()


def on_device(hidden_act, out_grad, weight, loss_mask, positions):
    t, f = hidden_act.shape
    n, b = out_grad.shape
    dma = pltpu.SemaphoreType.DMA
    vm = pltpu.VMEM
    return pl.pallas_call(
        kernel,
        out_shape=(pltpu.VMEM((t, f), BF16), pltpu.VMEM((f, b), BF16)),
        in_specs=[pl.BlockSpec(memory_space=pl.ANY)] * 5,
        out_specs=[pl.BlockSpec(memory_space=vm)] * 2,
        scratch_shapes=[
            vm((t, f), BF16),
            vm((n, b), BF16),
            vm((f, b), BF16),
            vm((16, 128), jnp.int32),
            vm((16, 128), jnp.int32),
            vm((n, b), BF16),
            vm((8, f, t), BF16),
            vm((NZ, 2, 2, n, b), BF16),
            vm((f, b), BF16),
            vm((f, b), BF16),
            vm((f, b), BF16),
            vm((f, b), F32),
            vm((NY, t, f), BF16),
            vm((NY, t, f), BF16),
            vm((NY, t, f), F32),
            vm((2, t // 2, f), BF16),
            vm((2, t // 2, f), BF16),
            vm((2, t, f), BF16),
            vm((2, t, f), BF16),
            dma((5,)),
            dma((2,)), dma((2,)),
            dma((6,)), dma((6,)),
            dma((8,)), dma((8,)),
            dma((1,)), dma((1,)),
            dma((16 * SUB,)), dma((16 * SUB,)),
            dma((16,)), dma((16,)),
            dma((CH,)), dma((CH,)),
            dma((8,)), dma((8,)),
            dma((2,)), dma((2,)),
            dma((4,)), dma((4,)),
        ],
        compiler_params=pltpu.CompilerParams(
            collective_id=0, has_side_effects=True, vmem_limit_bytes=VMEM_LIMIT
        ),
    )(hidden_act, out_grad, weight, loss_mask.reshape(-1, 128), positions.reshape(-1, 128))


def solution(mesh):
    return jax.shard_map(
        on_device,
        mesh=mesh,
        in_specs=(P("row", "col"), P("col", "row"), P("col", "row"), P(), P()),
        out_specs=(P("row", "col"), P("col", "row")),
        check_vma=False,
    )
```

```python
import contextlib

import jax
import jax.numpy as jnp
from jax import lax
from jax.experimental import pallas as pl
from jax.experimental.pallas import tpu as pltpu
from jax.sharding import PartitionSpec as P

MESH = pl.DeviceIdType.MESH
BF16 = jnp.bfloat16
F32 = jnp.float32
NY, NX, NZ = 4, 4, 8
scope = contextlib.nullcontext
VMEM_LIMIT = 62 * 2**20
YPOS = (1, 2, 4)
CH = 4


def local_token_scale(mask_ref, pos_ref, col, n_local):
    rows = pos_ref.shape[0]
    lane = lax.broadcasted_iota(jnp.int32, (n_local, 128), 1)
    sub = lax.broadcasted_iota(jnp.int32, (n_local, 128), 0)
    per = 128 // n_local
    mine_row = col // per
    offset = (col % per) * n_local
    pick = lane == sub + offset
    mine_pos = pos_ref[pl.ds(mine_row, 1), :]
    mine_mask = mask_ref[pl.ds(mine_row, 1), :]
    first = jnp.sum(jnp.where(pick, (mine_row * 128 + lane - mine_pos).astype(F32), 0.0), axis=1, keepdims=True)
    own_mask = jnp.sum(jnp.where(pick, mine_mask.astype(F32), 0.0), axis=1, keepdims=True)
    length = jnp.zeros((n_local, 128), F32)
    kept = jnp.zeros((n_local, 128), F32)
    for q in range(rows):
        begins = (q * 128 + lane - pos_ref[q : q + 1, :]).astype(F32)
        same = begins == first
        length = length + jnp.where(same, 1.0, 0.0)
        kept = kept + jnp.where(same, mask_ref[q : q + 1, :].astype(F32), 0.0)
    length = jnp.sum(length, axis=1, keepdims=True)
    kept = jnp.maximum(jnp.sum(kept, axis=1, keepdims=True), 1.0)
    return own_mask * length / kept


def dot_nn(a, b):
    return lax.dot_general(a, b, (((1,), (0,)), ((), ())), preferred_element_type=F32)


def dot_nt(a, b):
    return lax.dot_general(a, b, (((1,), (1,)), ((), ())), preferred_element_type=F32)


def kernel(
    hid_hbm, og_hbm, w_hbm, mask_hbm, pos_hbm, ig_ref, wg_ref,
    hid_ref, og_ref, w_ref, mask_ref, pos_ref,
    sc, hidt, S, wrecv, wg_send, wg_recv, wg_own, ig_send, ig_recv, ig_own, a_send, a_recv, b_send, b_recv,
    in_s, sc_s, sc_r, hy_s, hy_r, hx_s, hx_r, w_s, w_r, z_s, z_r, k_s, k_r, wg_s, wg_r, ig_s, ig_r, a_s, a_r, b_s, b_r,
):
    row = lax.axis_index("row")
    col = lax.axis_index("col")
    Y, x = row // NX, row % NX
    z, l, k = col // 4, (col // 2) % 2, col % 2
    dpx = x + 1 - 2 * (x % 2)
    tpx = 3 - x
    par, tpar = x // 2, 1 - x // 2
    g = ((x + 1) // 2) % 2
    lt = (z % 2 + g) % 2

    def dev(Y=Y, x=x, z=z, l=l, k=k):
        return (Y * NX + x, z * 4 + l * 2 + k)

    dp, tp, other = dev(x=dpx), dev(x=tpx), dev(k=1 - k)
    zdev = (dev(z=(z + 1) % NZ), dev(z=(z + NZ - 1) % NZ))
    zdev2 = (dev(z=(z + 2) % NZ), dev(z=(z + NZ - 2) % NZ))
    ydev = (dev(Y=(Y + 1) % NY), dev(Y=(Y + NY - 1) % NY))
    ldev, dpl = dev(l=1 - l), dev(x=dpx, l=1 - l)

    bar = pltpu.get_barrier_semaphore()
    peers = [dp, tp, other, *zdev, *zdev2, *ydev, ldev, dpl]
    for p in peers:
        pl.semaphore_signal(bar, inc=1, device_id=p, device_id_type=MESH)
    load = [
        pltpu.make_async_copy(a, b, in_s.at[i])
        for i, (a, b) in enumerate(
            [(mask_hbm, mask_ref), (pos_hbm, pos_ref), (og_hbm, og_ref), (hid_hbm, hid_ref), (w_hbm, w_ref)]
        )
    ]
    for c in load:
        c.start()

    sends = []

    def rc(src, dst, ss, rs, to):
        return pltpu.make_async_remote_copy(src, dst, ss, rs, device_id=to, device_id_type=MESH)

    def go(src, dst, ss, rs, to):
        c = rc(src, dst, ss, rs, to)
        c.start()
        sends.append(c)
        return c

    for c in load[:3]:
        c.wait()
    scale = local_token_scale(mask_ref, pos_ref, col, og_ref.shape[0])
    sc[...] = (og_ref[...].astype(F32) * scale).astype(BF16)
    pl.semaphore_wait(bar, len(peers))

    member = l == lt
    a_far = rc(sc, S.at[z, k, 1], sc_s.at[0], sc_r.at[1], dp)
    b_far = rc(sc, S.at[z, k, 1], sc_s.at[1], sc_r.at[1], dpl)
    b_near = rc(sc, S.at[z, k, 0], sc_s.at[1], sc_r.at[0], ldev)

    @pl.when(member)
    def _():
        b_near.start()
        S[z, k, 0] = sc[...]

    @pl.when(jnp.logical_not(member))
    def _():
        a_far.start()
        b_far.start()

    wc = go(w_hbm, wrecv, w_s.at[0], w_r.at[0], dp)
    myj = 2 * Y + par
    half = hid_ref.shape[1] // 2
    load[3].wait()
    hidt[myj] = hid_ref[...].T

    def hrows(j, h):
        return hidt.at[j, pl.ds(h * half, half)]

    def block_of(d, parity):
        return 2 * ((Y + d) % NY) + parity

    hy, hx, hf = {}, {}, {}

    def send_hx(d, h):
        r = hrows(block_of(d, par), h)
        hx[d, h] = go(r, r, hx_s.at[d * 2 + h], hx_r.at[d * 2 + h], tp)

    def send_own(h):
        for e in range(2):
            hy[e, h] = go(hrows(myj, h), hrows(myj, h), hy_s.at[e * 2 + h], hy_r.at[e * 2 + h], ydev[e])
        send_hx(0, h)

    send_own(0)

    def y_arrived(e, h):
        hy[e, h].wait_recv()
        if h == e:
            r = hrows(block_of((NY - 1, 1)[e], par), h)
            hf[e] = go(r, r, hy_s.at[4 + e], hy_r.at[4 + e], ydev[e])
        send_hx((NY - 1, 1)[e], h)

    a_far.wait_recv()

    kc, zc = {}, {}

    def to_core(zz, slot, idx):
        kc[idx, slot] = go(S.at[zz, k, slot], S.at[zz, k, slot], k_s.at[idx * 2 + slot], k_r.at[idx * 2 + slot], other)

    def origin_of(e, step):
        return (z + NZ - step) % NZ if e == 0 else (z + step) % NZ

    def hidden_step(i):
        for n in range(len(YPOS)):
            if YPOS[n] == i:
                if n < 2:
                    y_arrived(0, n)
                    y_arrived(1, n)
                else:
                    hf[0].wait_recv()
                    send_hx(2, 0)

    def z_hop(e, origin_step, sem_step, slot, to):
        i = (e * 4 + sem_step) * 2 + slot
        r = S.at[origin_of(e, origin_step), k, slot]
        zc[e, sem_step, slot] = go(r, r, z_s.at[i], z_r.at[i], to)

    for slot in (1, 0):
        if slot == 0:

            @pl.when(jnp.logical_not(member))
            def _():
                b_near.wait_recv()

        for e in range(2):
            z_hop(e, 0, 0, slot, zdev[e])
    for slot in (1, 0):
        for e in range(2):
            z_hop(e, 0, 1, slot, zdev2[e])
    send_own(1)
    for slot in (1, 0):
        to_core(z, slot, 0)
    for slot in (1, 0):
        for e in range(2):
            zc[e, 0, slot].wait_recv()
            to_core(origin_of(e, 1), slot, 1 if e == 0 else 5)
    hidden_step(1)
    for slot in (1, 0):
        for e in range(2):
            zc[e, 1, slot].wait_recv()
            z_hop(e, 2, 2, slot, zdev[e])
            if slot != e:
                z_hop(e, 2, 3, slot, zdev2[e])
            to_core(origin_of(e, 2), slot, 2 if e == 0 else 6)
        if slot == 1:
            hidden_step(2)
    hidden_step(3)
    for slot in (1, 0):
        for e in range(2):
            zc[e, 2, slot].wait_recv()
            to_core(origin_of(e, 3), slot, 3 if e == 0 else 7)
        if slot == 1:
            hidden_step(4)
    hidden_step(5)
    hf[1].wait_recv()
    send_hx(2, 1)
    for slot in (1, 0):
        zc[1 - slot, 3, slot].wait_recv()
        to_core(origin_of(1 - slot, 4), slot, 4)
    hidden_step(6)
    for slot in (1, 0):
        for i in range(8):
            kc[i, slot].wait_recv()

    load[4].wait()
    wc.wait_recv()

    def ig_block(d, parity):
        zz = block_of(d, parity)
        s0 = S[zz, :, 0].reshape(128, -1)
        s1 = S[zz, :, 1].reshape(128, -1)
        return dot_nt(s0, w_ref[...]) + dot_nt(s1, wrecv[...])

    igc, wgc = {}, {}

    def ig_partner(d):
        with scope(f"igp{d}"):
            ig_send[d] = ig_block(d, tpar).astype(BF16)

    def send_ig(d, q):
        r = pl.ds(q * 32, 32)
        igc[d, q] = go(ig_send.at[d, r], ig_recv.at[d, r], ig_s.at[d * 4 + q], ig_r.at[d * 4 + q], tp)

    rows = hid_ref.shape[1] // CH

    def lhs(c):
        return jnp.concatenate([hidt[j, c * rows : (c + 1) * rows] for j in range(2 * NY)], axis=1)

    def rhs(slot):
        return S[:, :, slot].reshape(1024, -1)

    def wg_partner(c):
        sl = pl.ds(c * rows, rows)
        with scope(f"wgp{c}"):
            wg_send[sl] = dot_nn(lhs(c), rhs(1)).astype(BF16)
        wgc[c] = go(wg_send.at[sl], wg_recv.at[sl], wg_s.at[c], wg_r.at[c], dp)

    ac, bc = {}, {}

    def arrived(d, q):
        igc[d, q].wait_recv()
        r = pl.ds(q * 32, 32)
        return ig_own[d, r] + ig_recv[d, r].astype(F32)

    def send_a(q):
        a_send[q] = arrived(2, q).astype(BF16)
        ac[q] = go(a_send.at[q], a_recv.at[q], a_s.at[q], a_r.at[q], ydev[q // 2])

    def send_b(d, q):
        e = d // 2
        r = pl.ds(q * 32, 32)
        value = arrived(d, q)
        if q // 2 == e:
            ac[q].wait_recv()
            value = value + a_recv[q].astype(F32)
        b_send[e, r] = value.astype(BF16)
        bc[e, q] = go(b_send.at[e, r], b_recv.at[e, r], b_s.at[e * 4 + q], b_r.at[e * 4 + q], ydev[e])

    def ig_own_block(d):
        ig_own[d] = ig_block(d, par)

    def wg_own_chunk(c):
        wg_own[c * rows : (c + 1) * rows] = dot_nn(lhs(c), rhs(0))

    def wg_done(c):
        wgc[c].wait_recv()
        sl = pl.ds(c * rows, rows)
        wg_ref[sl] = (wg_own[sl] + wg_recv[sl].astype(F32)).astype(BF16)

    ig_partner(2)
    for q in (0, 2, 1, 3):
        send_ig(2, q)
    for d in range(NY):
        hx[d, 0].wait_recv()
    for c in range(CH // 2):
        wg_partner(c)
    ig_partner(1)
    ig_partner(3)
    for d, q in ((1, 2), (3, 0), (1, 3), (3, 1), (1, 0), (3, 2), (1, 1), (3, 3)):
        send_ig(d, q)
    ig_own_block(2)
    ig_partner(0)
    for q in range(4):
        send_ig(0, q)
    ig_own_block(1)
    ig_own_block(3)
    for q in (0, 2, 1, 3):
        send_a(q)
    send_b(1, 2)
    send_b(3, 0)
    for d in range(NY):
        hx[d, 1].wait_recv()
    for c in range(CH // 2, CH):
        wg_partner(c)
    send_b(1, 3)
    send_b(3, 1)
    ig_own_block(0)
    for c in range(CH):
        wg_own_chunk(c)
    for q in range(2):
        send_b(1, q)
        send_b(3, 2 + q)
    for c in range(CH - 1):
        wg_done(c)
    for q in range(4):
        ig_own[0, q * 32 : (q + 1) * 32] = arrived(0, q)
    wg_done(CH - 1)
    for q in (2, 3, 0, 1):
        for e in range(2):
            bc[e, q].wait_recv()
    ig_ref[...] = (ig_own[0] + b_recv[0].astype(F32) + b_recv[1].astype(F32)).astype(BF16)

    b_near.wait_send()

    @pl.when(jnp.logical_not(member))
    def _():
        a_far.wait_send()

    for c in sends:
        c.wait_send()


def on_device(hidden_act, out_grad, weight, loss_mask, positions):
    t, f = hidden_act.shape
    n, b = out_grad.shape
    dma = pltpu.SemaphoreType.DMA
    vm = pltpu.VMEM
    return pl.pallas_call(
        kernel,
        out_shape=(pltpu.VMEM((t, f), BF16), pltpu.VMEM((f, b), BF16)),
        in_specs=[pl.BlockSpec(memory_space=pl.ANY)] * 5,
        out_specs=[pl.BlockSpec(memory_space=vm)] * 2,
        scratch_shapes=[
            vm((t, f), BF16),
            vm((n, b), BF16),
            vm((f, b), BF16),
            vm((16, 128), jnp.int32),
            vm((16, 128), jnp.int32),
            vm((n, b), BF16),
            vm((8, f, t), BF16),
            vm((NZ, 2, 2, n, b), BF16),
            vm((f, b), BF16),
            vm((f, b), BF16),
            vm((f, b), BF16),
            vm((f, b), F32),
            vm((NY, t, f), BF16),
            vm((NY, t, f), BF16),
            vm((NY, t, f), F32),
            vm((4, t // 4, f), BF16),
            vm((4, t // 4, f), BF16),
            vm((2, t, f), BF16),
            vm((2, t, f), BF16),
            dma((5,)),
            dma((2,)), dma((2,)),
            dma((6,)), dma((6,)),
            dma((8,)), dma((8,)),
            dma((1,)), dma((1,)),
            dma((16,)), dma((16,)),
            dma((16,)), dma((16,)),
            dma((CH,)), dma((CH,)),
            dma((16,)), dma((16,)),
            dma((4,)), dma((4,)),
            dma((8,)), dma((8,)),
        ],
        compiler_params=pltpu.CompilerParams(
            collective_id=0, has_side_effects=True, vmem_limit_bytes=VMEM_LIMIT
        ),
    )(hidden_act, out_grad, weight, loss_mask.reshape(-1, 128), positions.reshape(-1, 128))


def solution(mesh):
    return jax.shard_map(
        on_device,
        mesh=mesh,
        in_specs=(P("row", "col"), P("col", "row"), P("col", "row"), P(), P()),
        out_specs=(P("row", "col"), P("col", "row")),
        check_vma=False,
    )
```

```python
import contextlib

import jax
import jax.numpy as jnp
from jax import lax
from jax.experimental import pallas as pl
from jax.experimental.pallas import tpu as pltpu
from jax.sharding import PartitionSpec as P

MESH = pl.DeviceIdType.MESH
BF16 = jnp.bfloat16
F32 = jnp.float32
NY, NX, NZ = 4, 4, 8
scope = contextlib.nullcontext
VMEM_LIMIT = 62 * 2**20
YPOS = (1, 2, 4, 5)
YPOS_EARLY = (0, 0, 0, 0)
EARLY = 1
CH = 4


def local_token_scale(mask_ref, pos_ref, col, n_local):
    rows = pos_ref.shape[0]
    lane = lax.broadcasted_iota(jnp.int32, (n_local, 128), 1)
    sub = lax.broadcasted_iota(jnp.int32, (n_local, 128), 0)
    per = 128 // n_local
    mine_row = col // per
    offset = (col % per) * n_local
    pick = lane == sub + offset
    mine_pos = pos_ref[pl.ds(mine_row, 1), :]
    mine_mask = mask_ref[pl.ds(mine_row, 1), :]
    first = jnp.sum(jnp.where(pick, (mine_row * 128 + lane - mine_pos).astype(F32), 0.0), axis=1, keepdims=True)
    own_mask = jnp.sum(jnp.where(pick, mine_mask.astype(F32), 0.0), axis=1, keepdims=True)
    length = jnp.zeros((n_local, 128), F32)
    kept = jnp.zeros((n_local, 128), F32)
    for q in range(rows):
        begins = (q * 128 + lane - pos_ref[q : q + 1, :]).astype(F32)
        same = begins == first
        length = length + jnp.where(same, 1.0, 0.0)
        kept = kept + jnp.where(same, mask_ref[q : q + 1, :].astype(F32), 0.0)
    length = jnp.sum(length, axis=1, keepdims=True)
    kept = jnp.maximum(jnp.sum(kept, axis=1, keepdims=True), 1.0)
    return own_mask * length / kept


def dot_nn(a, b):
    return lax.dot_general(a, b, (((1,), (0,)), ((), ())), preferred_element_type=F32)


def dot_nt(a, b):
    return lax.dot_general(a, b, (((1,), (1,)), ((), ())), preferred_element_type=F32)


def kernel(
    hid_hbm, og_hbm, w_hbm, mask_hbm, pos_hbm, ig_ref, wg_ref,
    hid_ref, og_ref, w_ref, mask_ref, pos_ref,
    sc, hidt, S, wrecv, wg_send, wg_recv, wg_own, ig_send, ig_recv, ig_own, a_send, a_recv, b_send, b_recv,
    in_s, z_in, sc_s, sc_r, hy_s, hy_r, hx_s, hx_r, w_s, w_r, z_s, z_r, k_s, k_r, wg_s, wg_r, ig_s, ig_r, a_s, a_r, b_s, b_r,
):
    row = lax.axis_index("row")
    col = lax.axis_index("col")
    Y, x = row // NX, row % NX
    z, l, k = col // 4, (col // 2) % 2, col % 2
    dpx = x + 1 - 2 * (x % 2)
    tpx = 3 - x
    par, tpar = x // 2, 1 - x // 2
    g = ((x + 1) // 2) % 2
    lt = (z % 2 + g) % 2

    def dev(Y=Y, x=x, z=z, l=l, k=k):
        return (Y * NX + x, z * 4 + l * 2 + k)

    dp, tp, other = dev(x=dpx), dev(x=tpx), dev(k=1 - k)
    zdev = (dev(z=(z + 1) % NZ), dev(z=(z + NZ - 1) % NZ))
    zdev2 = (dev(z=(z + 2) % NZ), dev(z=(z + NZ - 2) % NZ))
    ydev = (dev(Y=(Y + 1) % NY), dev(Y=(Y + NY - 1) % NY))
    ldev, dpl = dev(l=1 - l), dev(x=dpx, l=1 - l)

    bar = pltpu.get_barrier_semaphore()
    peers = [dp, tp, other, *ydev, ldev, dpl]
    for p in peers:
        pl.semaphore_signal(bar, inc=1, device_id=p, device_id_type=MESH)
    zpeers = [(z + step) % NZ for step in (1, NZ - 1, 2, NZ - 2)]
    for zz in zpeers:

        @pl.when(zz > z)
        def _():
            pl.semaphore_signal(bar, inc=1, device_id=dev(z=zz), device_id_type=MESH)

    load = [
        pltpu.make_async_copy(a, b, in_s.at[i])
        for i, (a, b) in enumerate(
            [(mask_hbm, mask_ref), (pos_hbm, pos_ref), (og_hbm, og_ref), (hid_hbm, hid_ref), (w_hbm, w_ref)]
        )
    ]
    for c in load:
        c.start()

    sends = []

    def rc(src, dst, ss, rs, to):
        return pltpu.make_async_remote_copy(src, dst, ss, rs, device_id=to, device_id_type=MESH)

    def go(src, dst, ss, rs, to):
        c = rc(src, dst, ss, rs, to)
        c.start()
        sends.append(c)
        return c

    for c in load[:3]:
        c.wait()
    scale = local_token_scale(mask_ref, pos_ref, col, og_ref.shape[0])
    sc[...] = (og_ref[...].astype(F32) * scale).astype(BF16)
    below = sum(((zz < z).astype(jnp.int32) for zz in zpeers), 0)
    pl.semaphore_wait(bar, len(peers) + below)
    for zz in zpeers:

        @pl.when(zz < z)
        def _():
            pl.semaphore_signal(z_in, inc=1, device_id=dev(z=zz), device_id_type=MESH)


    member = l == lt
    a_far = rc(sc, S.at[z, k, 1], sc_s.at[0], sc_r.at[1], dp)
    b_far = rc(sc, S.at[z, k, 1], sc_s.at[1], sc_r.at[1], dpl)
    b_near = rc(sc, S.at[z, k, 0], sc_s.at[1], sc_r.at[0], ldev)

    @pl.when(member)
    def _():
        b_near.start()
        S[z, k, 0] = sc[...]

    @pl.when(jnp.logical_not(member))
    def _():
        a_far.start()
        b_far.start()

    wc = go(w_hbm, wrecv, w_s.at[0], w_r.at[0], dp)
    myj = 2 * Y + par
    half = hid_ref.shape[1] // 2
    load[3].wait()
    hidt[myj] = hid_ref[...].T

    def hrows(j, h):
        return hidt.at[j, pl.ds(h * half, half)]

    def block_of(d, parity):
        return 2 * ((Y + d) % NY) + parity

    hy, hx, hf = {}, {}, {}

    for d in range(NY):
        for h in range(2):
            r = hrows(block_of(d, par), h)
            hx[d, h] = rc(r, r, hx_s.at[d * 2 + h], hx_r.at[d * 2 + h], tp)
    for e in range(2):
        r = hrows(block_of((NY - 1, 1)[e], par), e)
        hf[e] = rc(r, r, hy_s.at[4 + e], hy_r.at[4 + e], ydev[e])
    sends.extend([*hx.values(), *hf.values()])

    def send_hx(d, h):
        hx[d, h].start()

    def send_own(h):
        for e in range(2):
            hy[e, h] = go(hrows(myj, h), hrows(myj, h), hy_s.at[e * 2 + h], hy_r.at[e * 2 + h], ydev[e])
        send_hx(0, h)

    send_own(0)

    def y_arrived(e, h):
        hy[e, h].wait_recv()
        if h == e:
            hf[e].start()
        hx[(NY - 1, 1)[e], h].start()

    a_far.wait_recv()

    kc, zc = {}, {}

    def to_core(zz, slot, idx):
        kc[idx, slot] = go(S.at[zz, k, slot], S.at[zz, k, slot], k_s.at[idx * 2 + slot], k_r.at[idx * 2 + slot], other)

    def origin_of(e, step):
        return (z + NZ - step) % NZ if e == 0 else (z + step) % NZ

    def hidden_step(i):
        for places, here in ((YPOS, z >= EARLY), (YPOS_EARLY, z < EARLY)):
            if i not in places:
                continue

            @pl.when(here)
            def _():
                for n in range(4):
                    if places[n] != i:
                        continue
                    if n < 2:
                        y_arrived(0, n)
                        y_arrived(1, n)
                    else:
                        hf[n - 2].wait_recv()
                        send_hx(2, n - 2)

    def z_hop(e, origin_step, sem_step, slot, to):
        i = (e * 4 + sem_step) * 2 + slot
        r = S.at[origin_of(e, origin_step), k, slot]
        zc[e, sem_step, slot] = go(r, r, z_s.at[i], z_r.at[i], to)

    @pl.when(below < len(zpeers))
    def _():
        pl.semaphore_wait(z_in, len(zpeers) - below)

    for slot in (1, 0):
        if slot == 0:

            @pl.when(jnp.logical_not(member))
            def _():
                b_near.wait_recv()

        for e in range(2):
            z_hop(e, 0, 0, slot, zdev[e])
    for slot in (1, 0):
        for e in range(2):
            z_hop(e, 0, 1, slot, zdev2[e])
    send_own(1)
    for slot in (1, 0):
        to_core(z, slot, 0)
    hidden_step(0)
    for slot in (1, 0):
        for e in range(2):
            zc[e, 0, slot].wait_recv()
            to_core(origin_of(e, 1), slot, 1 if e == 0 else 5)
    hidden_step(1)
    for slot in (1, 0):
        for e in range(2):
            zc[e, 1, slot].wait_recv()
            z_hop(e, 2, 2, slot, zdev[e])
            if slot != e:
                z_hop(e, 2, 3, slot, zdev2[e])
            to_core(origin_of(e, 2), slot, 2 if e == 0 else 6)
        if slot == 1:
            hidden_step(2)
    hidden_step(3)
    for slot in (1, 0):
        for e in range(2):
            zc[e, 2, slot].wait_recv()
            to_core(origin_of(e, 3), slot, 3 if e == 0 else 7)
        if slot == 1:
            hidden_step(4)
    hidden_step(5)
    for slot in (1, 0):
        zc[1 - slot, 3, slot].wait_recv()
        to_core(origin_of(1 - slot, 4), slot, 4)
    hidden_step(6)
    for slot in (1, 0):
        for i in range(8):
            kc[i, slot].wait_recv()

    load[4].wait()
    wc.wait_recv()

    def ig_block(d, parity):
        zz = block_of(d, parity)
        s0 = S[zz, :, 0].reshape(128, -1)
        s1 = S[zz, :, 1].reshape(128, -1)
        return dot_nt(s0, w_ref[...]) + dot_nt(s1, wrecv[...])

    igc, wgc = {}, {}

    def ig_partner(d):
        with scope(f"igp{d}"):
            ig_send[d] = ig_block(d, tpar).astype(BF16)

    def send_ig(d, q):
        r = pl.ds(q * 32, 32)
        igc[d, q] = go(ig_send.at[d, r], ig_recv.at[d, r], ig_s.at[d * 4 + q], ig_r.at[d * 4 + q], tp)

    rows = hid_ref.shape[1] // CH

    def lhs(c):
        return jnp.concatenate([hidt[j, c * rows : (c + 1) * rows] for j in range(2 * NY)], axis=1)

    def rhs(slot):
        return S[:, :, slot].reshape(1024, -1)

    def wg_partner(c):
        sl = pl.ds(c * rows, rows)
        with scope(f"wgp{c}"):
            wg_send[sl] = dot_nn(lhs(c), rhs(1)).astype(BF16)
        wgc[c] = go(wg_send.at[sl], wg_recv.at[sl], wg_s.at[c], wg_r.at[c], dp)

    ac, bc = {}, {}

    def arrived(d, q):
        igc[d, q].wait_recv()
        r = pl.ds(q * 32, 32)
        return ig_own[d, r] + ig_recv[d, r].astype(F32)

    def send_a(q):
        a_send[q] = arrived(2, q).astype(BF16)
        ac[q] = go(a_send.at[q], a_recv.at[q], a_s.at[q], a_r.at[q], ydev[q // 2])

    def send_b(d, q):
        e = d // 2
        r = pl.ds(q * 32, 32)
        value = arrived(d, q)
        if q // 2 == e:
            ac[q].wait_recv()
            value = value + a_recv[q].astype(F32)
        b_send[e, r] = value.astype(BF16)
        bc[e, q] = go(b_send.at[e, r], b_recv.at[e, r], b_s.at[e * 4 + q], b_r.at[e * 4 + q], ydev[e])

    def ig_own_block(d):
        ig_own[d] = ig_block(d, par)

    def wg_own_chunk(c):
        wg_own[c * rows : (c + 1) * rows] = dot_nn(lhs(c), rhs(0))

    def wg_done(c):
        wgc[c].wait_recv()
        sl = pl.ds(c * rows, rows)
        wg_ref[sl] = (wg_own[sl] + wg_recv[sl].astype(F32)).astype(BF16)

    ig_partner(2)
    for q in (0, 2, 1, 3):
        send_ig(2, q)
    for d in range(NY):
        hx[d, 0].wait_recv()
    for c in range(CH // 2):
        wg_partner(c)
    ig_partner(1)
    ig_partner(3)
    for d, q in ((1, 2), (3, 0), (1, 3), (3, 1), (1, 0), (3, 2), (1, 1), (3, 3)):
        send_ig(d, q)
    ig_own_block(2)
    ig_partner(0)
    for q in range(4):
        send_ig(0, q)
    ig_own_block(1)
    ig_own_block(3)
    for q in (0, 2, 1, 3):
        send_a(q)
    send_b(1, 2)
    send_b(3, 0)
    for d in range(NY):
        hx[d, 1].wait_recv()
    for c in range(CH // 2, CH):
        wg_partner(c)
    send_b(1, 3)
    send_b(3, 1)
    ig_own_block(0)
    for c in range(CH):
        wg_own_chunk(c)
    for q in range(2):
        send_b(1, q)
        send_b(3, 2 + q)
    for c in range(CH - 1):
        wg_done(c)
    for q in range(4):
        ig_own[0, q * 32 : (q + 1) * 32] = arrived(0, q)
    wg_done(CH - 1)
    for q in (2, 3, 0, 1):
        for e in range(2):
            bc[e, q].wait_recv()
    ig_ref[...] = (ig_own[0] + b_recv[0].astype(F32) + b_recv[1].astype(F32)).astype(BF16)

    b_near.wait_send()

    @pl.when(jnp.logical_not(member))
    def _():
        a_far.wait_send()

    for c in sends:
        c.wait_send()


def on_device(hidden_act, out_grad, weight, loss_mask, positions):
    t, f = hidden_act.shape
    n, b = out_grad.shape
    dma = pltpu.SemaphoreType.DMA
    vm = pltpu.VMEM
    return pl.pallas_call(
        kernel,
        out_shape=(pltpu.VMEM((t, f), BF16), pltpu.VMEM((f, b), BF16)),
        in_specs=[pl.BlockSpec(memory_space=pl.ANY)] * 5,
        out_specs=[pl.BlockSpec(memory_space=vm)] * 2,
        scratch_shapes=[
            vm((t, f), BF16),
            vm((n, b), BF16),
            vm((f, b), BF16),
            vm((16, 128), jnp.int32),
            vm((16, 128), jnp.int32),
            vm((n, b), BF16),
            vm((8, f, t), BF16),
            vm((NZ, 2, 2, n, b), BF16),
            vm((f, b), BF16),
            vm((f, b), BF16),
            vm((f, b), BF16),
            vm((f, b), F32),
            vm((NY, t, f), BF16),
            vm((NY, t, f), BF16),
            vm((NY, t, f), F32),
            vm((4, t // 4, f), BF16),
            vm((4, t // 4, f), BF16),
            vm((2, t, f), BF16),
            vm((2, t, f), BF16),
            dma((5,)),
            pltpu.SemaphoreType.REGULAR,
            dma((2,)), dma((2,)),
            dma((6,)), dma((6,)),
            dma((8,)), dma((8,)),
            dma((1,)), dma((1,)),
            dma((16,)), dma((16,)),
            dma((16,)), dma((16,)),
            dma((CH,)), dma((CH,)),
            dma((16,)), dma((16,)),
            dma((4,)), dma((4,)),
            dma((8,)), dma((8,)),
        ],
        compiler_params=pltpu.CompilerParams(
            collective_id=0, has_side_effects=True, vmem_limit_bytes=VMEM_LIMIT
        ),
    )(hidden_act, out_grad, weight, loss_mask.reshape(-1, 128), positions.reshape(-1, 128))


def solution(mesh):
    return jax.shard_map(
        on_device,
        mesh=mesh,
        in_specs=(P("row", "col"), P("col", "row"), P("col", "row"), P(), P()),
        out_specs=(P("row", "col"), P("col", "row")),
        check_vma=False,
    )
```

```python
import contextlib

import jax
import jax.numpy as jnp
from jax import lax
from jax.experimental import pallas as pl
from jax.experimental.pallas import tpu as pltpu
from jax.sharding import PartitionSpec as P

MESH = pl.DeviceIdType.MESH
BF16 = jnp.bfloat16
F32 = jnp.float32
NY, NX, NZ = 4, 4, 8
scope = contextlib.nullcontext
VMEM_LIMIT = 62 * 2**20
YPOS = (1, 1, 3, 4)
YPOS_EARLY = (0, 0, 0, 0)
EARLY = 1
CH = 4


def local_token_scale(mask_ref, pos_ref, col, n_local):
    rows = pos_ref.shape[0]
    lane = lax.broadcasted_iota(jnp.int32, (n_local, 128), 1)
    sub = lax.broadcasted_iota(jnp.int32, (n_local, 128), 0)
    per = 128 // n_local
    mine_row = col // per
    offset = (col % per) * n_local
    pick = lane == sub + offset
    mine_pos = pos_ref[pl.ds(mine_row, 1), :]
    mine_mask = mask_ref[pl.ds(mine_row, 1), :]
    first = jnp.sum(jnp.where(pick, (mine_row * 128 + lane - mine_pos).astype(F32), 0.0), axis=1, keepdims=True)
    own_mask = jnp.sum(jnp.where(pick, mine_mask.astype(F32), 0.0), axis=1, keepdims=True)
    length = jnp.zeros((n_local, 128), F32)
    kept = jnp.zeros((n_local, 128), F32)
    for q in range(rows):
        begins = (q * 128 + lane - pos_ref[q : q + 1, :]).astype(F32)
        same = begins == first
        length = length + jnp.where(same, 1.0, 0.0)
        kept = kept + jnp.where(same, mask_ref[q : q + 1, :].astype(F32), 0.0)
    length = jnp.sum(length, axis=1, keepdims=True)
    kept = jnp.maximum(jnp.sum(kept, axis=1, keepdims=True), 1.0)
    return own_mask * length / kept


def dot_nn(a, b):
    return lax.dot_general(a, b, (((1,), (0,)), ((), ())), preferred_element_type=F32)


def dot_nt(a, b):
    return lax.dot_general(a, b, (((1,), (1,)), ((), ())), preferred_element_type=F32)


def kernel(
    hid_hbm, og_hbm, w_hbm, mask_hbm, pos_hbm, ig_ref, wg_ref,
    hid_ref, og_ref, w_ref, mask_ref, pos_ref,
    sc, hidt, S, wrecv, wg_send, wg_recv, wg_own, ig_send, ig_recv, ig_own, a_send, a_recv, b_send, b_recv,
    in_s, z_in, sc_s, sc_r, hy_s, hy_r, hx_s, hx_r, w_s, w_r, z_s, z_r, k_s, k_r, wg_s, wg_r, ig_s, ig_r, a_s, a_r, b_s, b_r,
):
    row = lax.axis_index("row")
    col = lax.axis_index("col")
    Y, x = row // NX, row % NX
    z, l, k = col // 4, (col // 2) % 2, col % 2
    dpx = x + 1 - 2 * (x % 2)
    tpx = 3 - x
    par, tpar = x // 2, 1 - x // 2
    g = ((x + 1) // 2) % 2
    lt = (z % 2 + g) % 2

    def dev(Y=Y, x=x, z=z, l=l, k=k):
        return (Y * NX + x, z * 4 + l * 2 + k)

    dp, tp, other = dev(x=dpx), dev(x=tpx), dev(k=1 - k)
    zdev = (dev(z=(z + 1) % NZ), dev(z=(z + NZ - 1) % NZ))
    zdev2 = (dev(z=(z + 2) % NZ), dev(z=(z + NZ - 2) % NZ))
    ydev = (dev(Y=(Y + 1) % NY), dev(Y=(Y + NY - 1) % NY))
    ldev, dpl = dev(l=1 - l), dev(x=dpx, l=1 - l)

    bar = pltpu.get_barrier_semaphore()
    peers = [dp, tp, other, *ydev, ldev, dpl]
    for p in peers:
        pl.semaphore_signal(bar, inc=1, device_id=p, device_id_type=MESH)
    zpeers = [(z + step) % NZ for step in (1, NZ - 1, 2, NZ - 2)]
    for zz in zpeers:

        @pl.when(zz > z)
        def _():
            pl.semaphore_signal(bar, inc=1, device_id=dev(z=zz), device_id_type=MESH)

    load = [
        pltpu.make_async_copy(a, b, in_s.at[i])
        for i, (a, b) in enumerate(
            [(mask_hbm, mask_ref), (pos_hbm, pos_ref), (og_hbm, og_ref), (hid_hbm, hid_ref), (w_hbm, w_ref)]
        )
    ]
    for c in load:
        c.start()

    sends = []

    def rc(src, dst, ss, rs, to):
        return pltpu.make_async_remote_copy(src, dst, ss, rs, device_id=to, device_id_type=MESH)

    def go(src, dst, ss, rs, to):
        c = rc(src, dst, ss, rs, to)
        c.start()
        sends.append(c)
        return c

    for c in load[:3]:
        c.wait()
    scale = local_token_scale(mask_ref, pos_ref, col, og_ref.shape[0])
    sc[...] = (og_ref[...].astype(F32) * scale).astype(BF16)
    below = sum(((zz < z).astype(jnp.int32) for zz in zpeers), 0)
    pl.semaphore_wait(bar, len(peers) + below)
    for zz in zpeers:

        @pl.when(zz < z)
        def _():
            pl.semaphore_signal(z_in, inc=1, device_id=dev(z=zz), device_id_type=MESH)


    member = l == lt
    a_far = rc(sc, S.at[z, k, 1], sc_s.at[0], sc_r.at[1], dp)
    b_far = rc(sc, S.at[z, k, 1], sc_s.at[1], sc_r.at[1], dpl)
    b_near = rc(sc, S.at[z, k, 0], sc_s.at[1], sc_r.at[0], ldev)

    @pl.when(member)
    def _():
        b_near.start()
        S[z, k, 0] = sc[...]

    @pl.when(jnp.logical_not(member))
    def _():
        a_far.start()
        b_far.start()

    wc = go(w_hbm, wrecv, w_s.at[0], w_r.at[0], dp)
    myj = 2 * Y + par
    half = hid_ref.shape[1] // 2
    load[3].wait()
    hidt[myj] = hid_ref[...].T

    def hrows(j, h):
        return hidt.at[j, pl.ds(h * half, half)]

    def block_of(d, parity):
        return 2 * ((Y + d) % NY) + parity

    hy, hx, hf = {}, {}, {}

    for d in range(NY):
        for h in range(2):
            r = hrows(block_of(d, par), h)
            hx[d, h] = rc(r, r, hx_s.at[d * 2 + h], hx_r.at[d * 2 + h], tp)
    for e in range(2):
        r = hrows(block_of((NY - 1, 1)[e], par), e)
        hf[e] = rc(r, r, hy_s.at[4 + e], hy_r.at[4 + e], ydev[e])
    sends.extend([*hx.values(), *hf.values()])

    def send_hx(d, h):
        hx[d, h].start()

    def send_own(h):
        for e in range(2):
            hy[e, h] = go(hrows(myj, h), hrows(myj, h), hy_s.at[e * 2 + h], hy_r.at[e * 2 + h], ydev[e])
        send_hx(0, h)

    send_own(0)

    def y_arrived(e, h):
        hy[e, h].wait_recv()
        if h == e:
            hf[e].start()
        hx[(NY - 1, 1)[e], h].start()

    a_far.wait_recv()

    kc, zc = {}, {}

    def to_core(zz, slot, idx):
        kc[idx, slot] = go(S.at[zz, k, slot], S.at[zz, k, slot], k_s.at[idx * 2 + slot], k_r.at[idx * 2 + slot], other)

    def origin_of(e, step):
        return (z + NZ - step) % NZ if e == 0 else (z + step) % NZ

    def hidden_step(i):
        for places, here in ((YPOS, z >= EARLY), (YPOS_EARLY, z < EARLY)):
            if i not in places:
                continue

            @pl.when(here)
            def _():
                for n in range(4):
                    if places[n] != i:
                        continue
                    if n < 2:
                        y_arrived(0, n)
                        y_arrived(1, n)
                    else:
                        hf[n - 2].wait_recv()
                        send_hx(2, n - 2)

    def z_hop(e, origin_step, sem_step, slot, to):
        i = (e * 4 + sem_step) * 2 + slot
        r = S.at[origin_of(e, origin_step), k, slot]
        zc[e, sem_step, slot] = go(r, r, z_s.at[i], z_r.at[i], to)

    @pl.when(below < len(zpeers))
    def _():
        pl.semaphore_wait(z_in, len(zpeers) - below)

    for slot in (1, 0):
        if slot == 0:

            @pl.when(jnp.logical_not(member))
            def _():
                b_near.wait_recv()

        for e in range(2):
            z_hop(e, 0, 0, slot, zdev[e])
    for slot in (1, 0):
        for e in range(2):
            z_hop(e, 0, 1, slot, zdev2[e])
    send_own(1)
    for slot in (1, 0):
        to_core(z, slot, 0)
    hidden_step(0)
    for slot in (1, 0):
        for e in range(2):
            zc[e, 0, slot].wait_recv()
            to_core(origin_of(e, 1), slot, 1 if e == 0 else 5)
    hidden_step(1)
    for slot in (1, 0):
        for e in range(2):
            zc[e, 1, slot].wait_recv()
            z_hop(e, 2, 2, slot, zdev[e])
            if slot != e:
                z_hop(e, 2, 3, slot, zdev2[e])
            to_core(origin_of(e, 2), slot, 2 if e == 0 else 6)
        if slot == 1:
            hidden_step(2)
    hidden_step(3)
    for slot in (1, 0):
        for e in range(2):
            zc[e, 2, slot].wait_recv()
            to_core(origin_of(e, 3), slot, 3 if e == 0 else 7)
        if slot == 1:
            hidden_step(4)
    hidden_step(5)
    for slot in (1, 0):
        zc[1 - slot, 3, slot].wait_recv()
        to_core(origin_of(1 - slot, 4), slot, 4)
    hidden_step(6)
    for slot in (1, 0):
        for i in range(8):
            kc[i, slot].wait_recv()

    load[4].wait()
    wc.wait_recv()

    def ig_block(d, parity):
        zz = block_of(d, parity)
        s0 = S[zz, :, 0].reshape(128, -1)
        s1 = S[zz, :, 1].reshape(128, -1)
        return dot_nt(s0, w_ref[...]) + dot_nt(s1, wrecv[...])

    igc, wgc = {}, {}

    def ig_partner(d):
        with scope(f"igp{d}"):
            ig_send[d] = ig_block(d, tpar).astype(BF16)

    def send_ig(d, q):
        r = pl.ds(q * 32, 32)
        igc[d, q] = go(ig_send.at[d, r], ig_recv.at[d, r], ig_s.at[d * 4 + q], ig_r.at[d * 4 + q], tp)

    rows = hid_ref.shape[1] // CH

    def lhs(c):
        return jnp.concatenate([hidt[j, c * rows : (c + 1) * rows] for j in range(2 * NY)], axis=1)

    def rhs(slot):
        return S[:, :, slot].reshape(1024, -1)

    def wg_partner(c):
        sl = pl.ds(c * rows, rows)
        with scope(f"wgp{c}"):
            wg_send[sl] = dot_nn(lhs(c), rhs(1)).astype(BF16)
        wgc[c] = go(wg_send.at[sl], wg_recv.at[sl], wg_s.at[c], wg_r.at[c], dp)

    ac, bc = {}, {}

    def arrived(d, q):
        igc[d, q].wait_recv()
        r = pl.ds(q * 32, 32)
        return ig_own[d, r] + ig_recv[d, r].astype(F32)

    def send_a(q):
        a_send[q] = arrived(2, q).astype(BF16)
        ac[q] = go(a_send.at[q], a_recv.at[q], a_s.at[q], a_r.at[q], ydev[q // 2])

    def send_b(d, q):
        e = d // 2
        r = pl.ds(q * 32, 32)
        value = arrived(d, q)
        if q // 2 == e:
            ac[q].wait_recv()
            value = value + a_recv[q].astype(F32)
        b_send[e, r] = value.astype(BF16)
        bc[e, q] = go(b_send.at[e, r], b_recv.at[e, r], b_s.at[e * 4 + q], b_r.at[e * 4 + q], ydev[e])

    def ig_own_block(d):
        ig_own[d] = ig_block(d, par)

    def wg_own_chunk(c):
        wg_own[c * rows : (c + 1) * rows] = dot_nn(lhs(c), rhs(0))

    def wg_done(c):
        wgc[c].wait_recv()
        sl = pl.ds(c * rows, rows)
        wg_ref[sl] = (wg_own[sl] + wg_recv[sl].astype(F32)).astype(BF16)

    ig_partner(2)
    for q in (0, 2, 1, 3):
        send_ig(2, q)
    for d in range(NY):
        hx[d, 0].wait_recv()
    for c in range(CH // 2):
        wg_partner(c)
    ig_partner(1)
    ig_partner(3)
    for d, q in ((1, 2), (3, 0), (1, 3), (3, 1), (1, 0), (3, 2), (1, 1), (3, 3)):
        send_ig(d, q)
    ig_own_block(2)
    ig_partner(0)
    for q in range(4):
        send_ig(0, q)
    ig_own_block(1)
    ig_own_block(3)
    for q in (0, 2, 1, 3):
        send_a(q)
    send_b(1, 2)
    send_b(3, 0)
    for d in range(NY):
        hx[d, 1].wait_recv()
    for c in range(CH // 2, CH):
        wg_partner(c)
    send_b(1, 3)
    send_b(3, 1)
    ig_own_block(0)
    for c in range(CH):
        wg_own_chunk(c)
    for q in range(2):
        send_b(1, q)
        send_b(3, 2 + q)
    for c in range(CH - 1):
        wg_done(c)
    for q in range(4):
        ig_own[0, q * 32 : (q + 1) * 32] = arrived(0, q)
    wg_done(CH - 1)
    for q in (2, 3, 0, 1):
        for e in range(2):
            bc[e, q].wait_recv()
    ig_ref[...] = (ig_own[0] + b_recv[0].astype(F32) + b_recv[1].astype(F32)).astype(BF16)

    b_near.wait_send()

    @pl.when(jnp.logical_not(member))
    def _():
        a_far.wait_send()

    for c in sends:
        c.wait_send()


def on_device(hidden_act, out_grad, weight, loss_mask, positions):
    t, f = hidden_act.shape
    n, b = out_grad.shape
    dma = pltpu.SemaphoreType.DMA
    vm = pltpu.VMEM
    return pl.pallas_call(
        kernel,
        out_shape=(pltpu.VMEM((t, f), BF16), pltpu.VMEM((f, b), BF16)),
        in_specs=[pl.BlockSpec(memory_space=pl.ANY)] * 5,
        out_specs=[pl.BlockSpec(memory_space=vm)] * 2,
        scratch_shapes=[
            vm((t, f), BF16),
            vm((n, b), BF16),
            vm((f, b), BF16),
            vm((16, 128), jnp.int32),
            vm((16, 128), jnp.int32),
            vm((n, b), BF16),
            vm((8, f, t), BF16),
            vm((NZ, 2, 2, n, b), BF16),
            vm((f, b), BF16),
            vm((f, b), BF16),
            vm((f, b), BF16),
            vm((f, b), F32),
            vm((NY, t, f), BF16),
            vm((NY, t, f), BF16),
            vm((NY, t, f), F32),
            vm((4, t // 4, f), BF16),
            vm((4, t // 4, f), BF16),
            vm((2, t, f), BF16),
            vm((2, t, f), BF16),
            dma((5,)),
            pltpu.SemaphoreType.REGULAR,
            dma((2,)), dma((2,)),
            dma((6,)), dma((6,)),
            dma((8,)), dma((8,)),
            dma((1,)), dma((1,)),
            dma((16,)), dma((16,)),
            dma((16,)), dma((16,)),
            dma((CH,)), dma((CH,)),
            dma((16,)), dma((16,)),
            dma((4,)), dma((4,)),
            dma((8,)), dma((8,)),
        ],
        compiler_params=pltpu.CompilerParams(
            collective_id=0, has_side_effects=True, vmem_limit_bytes=VMEM_LIMIT
        ),
    )(hidden_act, out_grad, weight, loss_mask.reshape(-1, 128), positions.reshape(-1, 128))


def solution(mesh):
    return jax.shard_map(
        on_device,
        mesh=mesh,
        in_specs=(P("row", "col"), P("col", "row"), P("col", "row"), P(), P()),
        out_specs=(P("row", "col"), P("col", "row")),
        check_vma=False,
    )
```
